128 devices in a mesh: row: 4 (over y), col: 4 (over x_lo, core), depth: 8 (over x_hi, z).
Axes of the slice: x: 4 (x_hi: 2, x_lo: 2; x = x_hi * 2 + x_lo), y: 4, z: 4, core: 2. Of those that a mesh axis runs over, the one named last changes fastest.
Arguments:
- inputs: bfloat16 [2048, 12288], P('col', ('row', 'depth')), may hold values from -0.23925781 to 0.23925781
- weight_in: bfloat16 [12288, 24576], P(('row', 'depth'), 'col'), may hold values from -0.0546875 to 0.0546875
- saved_pre: bfloat16 [2048, 24576], P(('row', 'depth'), 'col'), may hold values from -10 to 10
- grad_hidden: bfloat16 [2048, 24576], P(('row', 'depth'), 'col'), may hold values from -6 to 6
Outputs:
- grad_inputs: bfloat16 [2048, 12288], P('col', ('row', 'depth'))
- grad_weight: bfloat16 [12288, 24576], P(('row', 'depth'), 'col')
The draws below stay inside these ranges and needn't reach their ends.
All inputs are finite; a program needn't handle non-finite values.
Results may differ from the reference program's by a relative error of at most 0.0049.
Values may be sent and summed in bfloat16 or wider, within the bound.
A program may use at most 192 MiB of HBM per device.

```python
import jax
import jax.numpy as jnp

D = 12288
FFW = 24576
TOKENS = 2048


def block_scale(rng, shape, split, smallest, largest):
    def one(axis_at, parts):
        draws = jax.random.uniform(jax.random.fold_in(jax.random.fold_in(rng, 6), axis_at), (parts,), jnp.float32, smallest / len(split), largest / len(split))
        return jnp.repeat(jnp.exp(draws), shape[axis_at] // parts).reshape((-1,) + (1,) * (len(shape) - axis_at - 1))

    level = one(*split[0])
    for cut in split[1:]:
        level = level * one(*cut)
    return level


def scatter_about(own_key, shape, scale, bound, shards=(), held_as=jnp.bfloat16):
    result = scale * jax.random.normal(own_key, shape, jnp.float32)
    if shards:
        result = result * block_scale(own_key, shape, shards, -0.22, 0.18)
    return jnp.clip(result, -bound, bound).astype(held_as)


def setup_inputs(seed: int = 0) -> dict:
    keys = jax.random.split(jax.random.key(seed), 5)
    inputs = scatter_about(keys[0], (TOKENS, D), 0.04, 0.23925781, ((0, 4), (1, 32)))
    weight_in = scatter_about(keys[1], (D, FFW), D ** -0.5, 0.0546875, ((0, 32), (1, 4)))
    saved_pre = scatter_about(keys[2], (TOKENS, FFW), 2.0, 10.0, ((0, 32), (1, 4)))
    grad_hidden = scatter_about(keys[3], (TOKENS, FFW), 1.0, 6.0, ((0, 32), (1, 4)))
    return dict(inputs=inputs, weight_in=weight_in, saved_pre=saved_pre, grad_hidden=grad_hidden)


def gelu_back(grad_hidden, saved_pre):
    pre = saved_pre.astype(jnp.float32)
    value, pull = jax.vjp(lambda a: jax.nn.gelu(a, approximate=True), pre)
    return pull(grad_hidden.astype(jnp.float32))[0].astype(jnp.bfloat16)

def reference(inputs, weight_in, saved_pre, grad_hidden):
    grad_pre = gelu_back(grad_hidden, saved_pre)
    grad_inputs = jnp.dot(grad_pre, weight_in.T, preferred_element_type=jnp.float32).astype(jnp.bfloat16)
    grad_weight = jnp.dot(inputs.T, grad_pre, preferred_element_type=jnp.float32).astype(jnp.bfloat16)
    return (grad_inputs, grad_weight)
```

```python
import functools

import jax
import jax.numpy as jnp
from jax import lax
from jax.experimental import pallas as pl
from jax.experimental.pallas import tpu as pltpu
from jax.sharding import PartitionSpec as P

MESH = pl.DeviceIdType.MESH
WIDTH = 256
ROOT = 0.7978845608028654
CUBE = 0.044715


def gelu_back(grad_hidden, saved_pre):
    a = saved_pre.astype(jnp.float32)
    square = a * a
    t = jnp.tanh(ROOT * (a + CUBE * (square * a)))
    slope = 0.5 * (1.0 + t) + 0.5 * a * (1.0 - t * t) * (ROOT * (1.0 + (3.0 * CUBE) * square))
    return (grad_hidden.astype(jnp.float32) * slope).astype(jnp.bfloat16)


def kernel(ticks, x_ref, pre_ref, gh_ref, w_hbm, dx_ref, dw_hbm, gall, wv, xt, acc, dwv, from_core, to_side, from_side,
           g_send, g_recv, p_send, p_recv, x_send, x_recv, r_send, r_recv, w_sem, o_sem):
    y = lax.axis_index("row")
    col = lax.axis_index("col")
    depth = lax.axis_index("depth")
    side, core = col // 2, col % 2
    far, z = depth // 4, depth % 4
    y_up, y_down = (y + 1) % 4, (y + 3) % 4
    z_up, z_down = (z + 1) % 4, (z + 3) % 4
    y_dev = ((y_up, col, depth), (y_down, col, depth))
    z_dev = ((y, col, far * 4 + z_up), (y, col, far * 4 + z_down))
    far_dev = (y, col, (1 - far) * 4 + z)
    side_dev = (y, (1 - side) * 2 + core, depth)
    core_dev = (y, side * 2 + 1 - core, depth)
    rows, model = x_ref.shape
    pair = 2 * WIDTH

    load_w = pltpu.make_async_copy(w_hbm, wv, w_sem)
    load_w.start()

    barrier = pltpu.get_barrier_semaphore()
    for dev in (*y_dev, *z_dev, far_dev, side_dev, core_dev):
        pl.semaphore_signal(barrier, 1, device_id=dev, device_id_type=MESH)
    pl.semaphore_wait(barrier, 7)

    def remote(src, dst, send, recv, dev):
        return pltpu.make_async_remote_copy(src, dst, send, recv, device_id=dev, device_id_type=MESH)

    def far_copy(t, which):
        return remote(
            gall.at[t, :, y, far, z], gall.at[t, :, y, which, z], p_send.at[t], p_recv.at[t], far_dev
        )

    def places(t, stage, chunk, way):
        up = way == 0
        if chunk == 0:
            first_in, first_out = (y_down, y_up) if up else (y_up, y_down)
            second_in = z_down if up else z_up
            if stage == 0:
                return gall.at[t, 0, y, :, z], gall.at[t, 0, first_in, :, z], y_dev[way]
            if stage == 1:
                return gall.at[t, 0, first_in, way, z], gall.at[t, 0, (y + 2) % 4, way, z], y_dev[way]
            if stage == 2:
                return gall.at[t, 0, :, :, z], gall.at[t, 0, :, :, second_in], z_dev[way]
            return gall.at[t, 0, :, way, second_in], gall.at[t, 0, :, way, (z + 2) % 4], z_dev[way]
        first_in = z_down if up else z_up
        second_in = y_down if up else y_up
        if stage == 0:
            return gall.at[t, 1, y, :, z], gall.at[t, 1, y, :, first_in], z_dev[way]
        if stage == 1:
            return gall.at[t, 1, y, way, first_in], gall.at[t, 1, y, way, (z + 2) % 4], z_dev[way]
        if stage == 2:
            return gall.at[t, 1, y], gall.at[t, 1, second_in], y_dev[way]
        return gall.at[t, 1, second_in, way], gall.at[t, 1, (y + 2) % 4, way], y_dev[way]

    def start(t, stage):
        for chunk in range(2):
            for way in range(2):
                out, _, dev = places(t, stage, chunk, way)
                remote(out, out, g_send.at[t, stage, chunk, way], g_recv.at[t, stage, chunk, way], dev).start()

    def arrive(t, stage):
        for chunk in range(2):
            for way in range(2):
                _, come, dev = places(t, stage, chunk, way)
                remote(come, come, g_send.at[t, stage, chunk, way], g_recv.at[t, stage, chunk, way], dev).wait_recv()

    def sent(t, stage):
        for chunk in range(2):
            for way in range(2):
                out, _, dev = places(t, stage, chunk, way)
                remote(out, out, g_send.at[t, stage, chunk, way], g_recv.at[t, stage, chunk, way], dev).wait_send()

    def own_grad(t, carry):
        for chunk in range(2):
            cols = pl.ds(pl.multiple_of(t * pair + chunk * WIDTH, WIDTH), WIDTH)
            gall[t, chunk, y, far, z] = gelu_back(gh_ref[:, cols], pre_ref[:, cols])
        far_copy(t, far).start()
        return carry

    lax.fori_loop(0, ticks, own_grad, 0)

    own = pl.ds(pl.multiple_of(col * rows, rows), rows)
    beside = pl.ds(pl.multiple_of(((1 - side) * 2 + core) * rows, rows), rows)
    near = pl.ds(pl.multiple_of((side * 2 + 1 - core) * rows, rows), rows)
    cross = pl.ds(pl.multiple_of(((1 - side) * 2 + 1 - core) * rows, rows), rows)
    xt[:, own] = x_ref[...].T
    x_side = remote(xt.at[:, own], xt.at[:, own], x_send.at[0], x_recv.at[0], side_dev)
    x_core = remote(xt.at[:, own], xt.at[:, own], x_send.at[1], x_recv.at[1], core_dev)
    x_cross = remote(xt.at[:, beside], xt.at[:, beside], x_send.at[2], x_recv.at[2], core_dev)
    x_side.start()
    x_core.start()

    acc[...] = jnp.zeros_like(acc)

    def dx_part(t, owner):
        total = acc[owner]
        for chunk in range(2):
            cols = pl.ds(pl.multiple_of(t * pair + chunk * WIDTH, WIDTH), WIDTH)
            g = gall[t, chunk, owner].reshape(rows, WIDTH)
            total += lax.dot_general(g, wv[:, cols], (((1,), (1,)), ((), ())), preferred_element_type=jnp.float32)
        acc[owner] = total

    def dw_store(t):
        cols = pl.ds(pl.multiple_of(t * pair, pair), pair)
        return pltpu.make_async_copy(dwv.at[t], dw_hbm.at[:, cols], o_sem.at[t])

    def dw_part(t):
        for chunk in range(2):
            g = gall[t, chunk].reshape(4 * rows, WIDTH)
            dwv[t, :, pl.ds(chunk * WIDTH, WIDTH)] = jnp.dot(
                xt[...], g, preferred_element_type=jnp.float32
            ).astype(jnp.bfloat16)
        dw_store(t).start()

    def advance(t):
        @pl.when(t + 3 < ticks)
        def _():
            far_copy(t + 3, 1 - far).wait_recv()
            start(t + 3, 0)

        @pl.when(t >= 0)
        def _():
            arrive(t, 2)
            start(t, 3)

        @pl.when(jnp.logical_and(t + 1 >= 0, t + 1 < ticks))
        def _():
            arrive(t + 1, 1)
            start(t + 1, 2)

        @pl.when(jnp.logical_and(t + 2 >= 0, t + 2 < ticks))
        def _():
            arrive(t + 2, 0)
            start(t + 2, 1)

    def fill(i, carry):
        advance(i - 3)
        return carry

    lax.fori_loop(0, 3, fill, 0)

    beside_in = remote(xt.at[:, beside], xt.at[:, beside], x_send.at[0], x_recv.at[0], side_dev)
    near_in = remote(xt.at[:, near], xt.at[:, near], x_send.at[1], x_recv.at[1], core_dev)
    cross_in = remote(xt.at[:, cross], xt.at[:, cross], x_send.at[2], x_recv.at[2], core_dev)
    beside_in.wait_recv()
    x_cross.start()
    near_in.wait_recv()
    cross_in.wait_recv()
    load_w.wait()

    def tick(t, carry):
        advance(t)
        arrive(t, 3)

        def one(owner, c):
            dx_part(t, owner)
            return c

        lax.fori_loop(0, 4, one, 0)
        dw_part(t)
        return carry

    lax.fori_loop(0, ticks - 1, tick, 0)

    last = ticks - 1
    advance(last)
    arrive(last, 3)

    def owner_of(s, c):
        return s * 2 + c

    give = []
    for k, s in enumerate((1 - side, side)):
        j = owner_of(s, 1 - core)
        dx_part(last, j)
        copy = remote(acc.at[j], from_core.at[k], r_send.at[k], r_recv.at[k], core_dev)
        copy.start()
        give.append(copy)
    dx_part(last, owner_of(1 - side, core))
    give[0].wait_recv()
    to_side[...] = (acc[owner_of(1 - side, core)] + from_core[0]).astype(jnp.bfloat16)
    across = remote(to_side, from_side, r_send.at[2], r_recv.at[2], side_dev)
    across.start()
    dx_part(last, owner_of(side, core))
    dw_part(last)
    give[1].wait_recv()
    across.wait_recv()
    dx_ref[...] = (acc[owner_of(side, core)] + from_core[1] + from_side[...].astype(jnp.float32)).astype(jnp.bfloat16)

    def finish(t, carry):
        far_copy(t, far).wait_send()
        for stage in range(4):
            sent(t, stage)
        dw_store(t).wait()
        return carry

    lax.fori_loop(0, ticks, finish, 0)
    x_side.wait_send()
    x_core.wait_send()
    x_cross.wait_send()
    for copy in give:
        copy.wait_send()
    across.wait_send()


def local(inputs, weight_in, saved_pre, grad_hidden):
    rows, model = inputs.shape
    tokens, hidden = saved_pre.shape
    ticks = hidden // (2 * WIDTH)
    vmem = pl.BlockSpec(memory_space=pltpu.VMEM)
    hbm = pl.BlockSpec(memory_space=pl.ANY)
    dma = pltpu.SemaphoreType.DMA
    return pl.pallas_call(
        functools.partial(kernel, ticks),
        out_shape=(
            jax.ShapeDtypeStruct((rows, model), jnp.bfloat16),
            jax.ShapeDtypeStruct((model, hidden), jnp.bfloat16),
        ),
        in_specs=[vmem, vmem, vmem, hbm],
        out_specs=(vmem, hbm),
        scratch_shapes=[
            pltpu.VMEM((ticks, 2, 4, 2, 4, tokens, WIDTH), jnp.bfloat16),
            pltpu.VMEM((model, hidden), jnp.bfloat16),
            pltpu.VMEM((model, 4 * rows), jnp.bfloat16),
            pltpu.VMEM((4, rows, model), jnp.float32),
            pltpu.VMEM((ticks, model, 2 * WIDTH), jnp.bfloat16),
            pltpu.VMEM((2, rows, model), jnp.float32),
            pltpu.VMEM((rows, model), jnp.bfloat16),
            pltpu.VMEM((rows, model), jnp.bfloat16),
            dma((ticks, 4, 2, 2)),
            dma((ticks, 4, 2, 2)),
            dma((ticks,)),
            dma((ticks,)),
            dma((3,)),
            dma((3,)),
            dma((3,)),
            dma((3,)),
            dma,
            dma((ticks,)),
        ],
        compiler_params=pltpu.CompilerParams(
            collective_id=0, has_side_effects=True, vmem_limit_bytes=60 * 2**20
        ),
        name="gather_and_multiply",
    )(inputs, saved_pre, grad_hidden, weight_in)


def solution(mesh):
    return jax.shard_map(
        local,
        mesh=mesh,
        in_specs=(
            P("col", ("row", "depth")),
            P(("row", "depth"), "col"),
            P(("row", "depth"), "col"),
            P(("row", "depth"), "col"),
        ),
        out_specs=(P("col", ("row", "depth")), P(("row", "depth"), "col")),
        check_vma=False,
    )
```

```python
import functools

import jax
import jax.numpy as jnp
from jax import lax
from jax.experimental import pallas as pl
from jax.experimental.pallas import tpu as pltpu
from jax.sharding import PartitionSpec as P

MESH = pl.DeviceIdType.MESH
WIDTH = 256
LEAD = (3, 2, 1, 0)
LAG = 1
PAIRED = 3
BEFORE = 2
ROOT = 0.7978845608028654
CUBE = 0.044715


def gelu_back(grad_hidden, saved_pre):
    a = saved_pre.astype(jnp.float32)
    square = a * a
    t = jnp.tanh(ROOT * (a + CUBE * (square * a)))
    slope = 0.5 * (1.0 + t) + 0.5 * a * (1.0 - t * t) * (ROOT * (1.0 + (3.0 * CUBE) * square))
    return (grad_hidden.astype(jnp.float32) * slope).astype(jnp.bfloat16)


def kernel(ticks, x_ref, pre_ref, gh_ref, w_hbm, dx_ref, dw_hbm, gall, gout, wv, wp, xt, xtp, acc, accp, dwv, dwp,
           from_core, from_core_p, to_chips, from_chips, g_send, g_recv, p_send, p_recv, x_send, x_recv, r_send, r_recv,
           wp_send, wp_recv, dwp_send, dwp_recv, w_sem, o_sem):
    y = lax.axis_index("row")
    col = lax.axis_index("col")
    depth = lax.axis_index("depth")
    side, core = col // 2, col % 2
    far, z = depth // 4, depth % 4
    y_up, y_down = (y + 1) % 4, (y + 3) % 4
    z_up, z_down = (z + 1) % 4, (z + 3) % 4
    y_dev = ((y_up, col, depth), (y_down, col, depth))
    z_dev = ((y, col, far * 4 + z_up), (y, col, far * 4 + z_down))
    far_dev = (y, col, (1 - far) * 4 + z)
    side_dev = (y, (1 - side) * 2 + core, depth)
    core_dev = (y, side * 2 + 1 - core, depth)
    diag_dev = (y, (1 - side) * 2 + core, (1 - far) * 4 + z)
    rows, model = x_ref.shape
    pair = 2 * WIDTH

    load_w = pltpu.make_async_copy(w_hbm, wv, w_sem)
    load_w.start()

    barrier = pltpu.get_barrier_semaphore()
    for dev in (*y_dev, *z_dev, far_dev, side_dev, core_dev, diag_dev):
        pl.semaphore_signal(barrier, 1, device_id=dev, device_id_type=MESH)
    pl.semaphore_wait(barrier, 8)

    def remote(src, dst, send, recv, dev):
        return pltpu.make_async_remote_copy(src, dst, send, recv, device_id=dev, device_id_type=MESH)

    def far_in(t):
        place = gall.at[t, :, y, 1 - far, z]
        return remote(place, place, p_send.at[t], p_recv.at[t], far_dev)

    def early(t):
        return pl.multiple_of(t * pair, pair)

    def mine(t):
        return pl.multiple_of((t + far * PAIRED) * pair, pair)

    def theirs(t):
        return pl.multiple_of((t + (1 - far) * PAIRED) * pair, pair)

    def late(t):
        return pl.multiple_of((t + PAIRED) * pair, pair)

    def places(t, stage, chunk, way):
        up = way == 0
        if chunk == 0:
            first_in, first_out = (y_down, y_up) if up else (y_up, y_down)
            second_in = z_down if up else z_up
            if stage == 0:
                return gall.at[t, 0, y, :, z], gall.at[t, 0, first_in, :, z], y_dev[way]
            if stage == 1:
                return gall.at[t, 0, first_in, way, z], gall.at[t, 0, (y + 2) % 4, way, z], y_dev[way]
            if stage == 2:
                return gall.at[t, 0, :, :, z], gall.at[t, 0, :, :, second_in], z_dev[way]
            return gall.at[t, 0, :, way, second_in], gall.at[t, 0, :, way, (z + 2) % 4], z_dev[way]
        first_in = z_down if up else z_up
        second_in = y_down if up else y_up
        if stage == 0:
            return gall.at[t, 1, y, :, z], gall.at[t, 1, y, :, first_in], z_dev[way]
        if stage == 1:
            return gall.at[t, 1, y, way, first_in], gall.at[t, 1, y, way, (z + 2) % 4], z_dev[way]
        if stage == 2:
            return gall.at[t, 1, y], gall.at[t, 1, second_in], y_dev[way]
        return gall.at[t, 1, second_in, way], gall.at[t, 1, (y + 2) % 4, way], y_dev[way]

    def start(t, stage):
        for chunk in range(2):
            for way in range(2):
                out, _, dev = places(t, stage, chunk, way)
                remote(out, out, g_send.at[t, stage, chunk, way], g_recv.at[t, stage, chunk, way], dev).start()

    def arrive(t, stage):
        for chunk in range(2):
            for way in range(2):
                _, come, dev = places(t, stage, chunk, way)
                remote(come, come, g_send.at[t, stage, chunk, way], g_recv.at[t, stage, chunk, way], dev).wait_recv()

    def sent(t, stage):
        for chunk in range(2):
            for way in range(2):
                out, _, dev = places(t, stage, chunk, way)
                remote(out, out, g_send.at[t, stage, chunk, way], g_recv.at[t, stage, chunk, way], dev).wait_send()

    def grad_at(base, chunk):
        cols = pl.ds(pl.multiple_of(base + chunk * WIDTH, WIDTH), WIDTH)
        return gelu_back(gh_ref[:, cols], pre_ref[:, cols])

    def own_grad(place, t, carry):
        for chunk in range(2):
            gall[t, chunk, y, far, z] = grad_at(place(t), chunk)
        out = gall.at[t, :, y, far, z]
        remote(out, out, p_send.at[t], p_recv.at[t], far_dev).start()
        return carry

    def paired_grad(t, carry):
        for chunk in range(2):
            gout[t - BEFORE, chunk] = grad_at(theirs(t), chunk)
        remote(gout.at[t - BEFORE], gall.at[t, :, y, far, z], p_send.at[t], p_recv.at[t], far_dev).start()
        for chunk in range(2):
            gall[t, chunk, y, far, z] = grad_at(mine(t), chunk)
        return carry

    after = BEFORE + PAIRED
    lax.fori_loop(0, BEFORE, functools.partial(own_grad, early), 0)
    lax.fori_loop(BEFORE, after, paired_grad, 0)
    lax.fori_loop(after, ticks, functools.partial(own_grad, late), 0)

    own = pl.ds(pl.multiple_of(col * rows, rows), rows)
    beside = pl.ds(pl.multiple_of(((1 - side) * 2 + core) * rows, rows), rows)
    near = pl.ds(pl.multiple_of((side * 2 + 1 - core) * rows, rows), rows)
    cross = pl.ds(pl.multiple_of(((1 - side) * 2 + 1 - core) * rows, rows), rows)
    xt[:, own] = x_ref[...].T

    def x_copy(k, src, dst, dev):
        return remote(src, dst, x_send.at[k], x_recv.at[k], dev)

    x_out = [
        x_copy(0, xt.at[:, own], xt.at[:, own], side_dev),
        x_copy(1, xt.at[:, own], xt.at[:, own], core_dev),
        x_copy(2, xt.at[:, own], xtp.at[:, own], far_dev),
        x_copy(3, xt.at[:, own], xtp.at[:, own], diag_dev),
        x_copy(4, xt.at[:, beside], xt.at[:, beside], core_dev),
        x_copy(5, xtp.at[:, own], xtp.at[:, own], core_dev),
        x_copy(6, xtp.at[:, beside], xtp.at[:, beside], core_dev),
    ]
    x_in = [
        x_copy(0, xt.at[:, beside], xt.at[:, beside], side_dev),
        x_copy(1, xt.at[:, near], xt.at[:, near], core_dev),
        x_copy(2, xtp.at[:, own], xtp.at[:, own], far_dev),
        x_copy(3, xtp.at[:, beside], xtp.at[:, beside], diag_dev),
        x_copy(4, xt.at[:, cross], xt.at[:, cross], core_dev),
        x_copy(5, xtp.at[:, near], xtp.at[:, near], core_dev),
        x_copy(6, xtp.at[:, cross], xtp.at[:, cross], core_dev),
    ]
    for copy in x_out[:4]:
        copy.start()

    def wp_copy(k):
        return remote(
            w_hbm.at[:, pl.ds(theirs(k + BEFORE), pair)], wp.at[k], wp_send.at[k], wp_recv.at[k], far_dev
        )

    def send_weights(k, carry):
        wp_copy(k).start()
        return carry

    lax.fori_loop(0, PAIRED, send_weights, 0)

    accp[...] = jnp.zeros_like(accp)
    acc[...] = jnp.zeros_like(acc)

    def dx_part(t, base, owner):
        total = acc[owner]
        for chunk in range(2):
            cols = pl.ds(pl.multiple_of(base + chunk * WIDTH, WIDTH), WIDTH)
            g = gall[t, chunk, owner].reshape(rows, WIDTH)
            total += lax.dot_general(g, wv[:, cols], (((1,), (1,)), ((), ())), preferred_element_type=jnp.float32)
        acc[owner] = total

    def dxp_part(t, owner):
        total = accp[owner]
        for chunk in range(2):
            w = wp[t - BEFORE, :, pl.ds(chunk * WIDTH, WIDTH)]
            g = gall[t, chunk, owner].reshape(rows, WIDTH)
            total += lax.dot_general(g, w, (((1,), (1,)), ((), ())), preferred_element_type=jnp.float32)
        accp[owner] = total

    def dw_store(t, base):
        return pltpu.make_async_copy(dwv.at[t], dw_hbm.at[:, pl.ds(base, pair)], o_sem.at[t])

    def dw_part(t, base):
        for chunk in range(2):
            g = gall[t, chunk].reshape(4 * rows, WIDTH)
            dwv[t, :, pl.ds(chunk * WIDTH, WIDTH)] = jnp.dot(
                xt[...], g, preferred_element_type=jnp.float32
            ).astype(jnp.bfloat16)
        dw_store(t, base).start()

    def dwp_copy(t, base):
        k = t - BEFORE
        return remote(dwp.at[k], dw_hbm.at[:, pl.ds(base, pair)], dwp_send.at[k], dwp_recv.at[k], far_dev)

    def dwp_part(t):
        for chunk in range(2):
            g = gall[t, chunk].reshape(4 * rows, WIDTH)
            dwp[t - BEFORE, :, pl.ds(chunk * WIDTH, WIDTH)] = jnp.dot(
                xtp[...], g, preferred_element_type=jnp.float32
            ).astype(jnp.bfloat16)
        dwp_copy(t, mine(t)).start()

    def advance(i):
        @pl.when(i + LEAD[0] < ticks)
        def _():
            far_in(i + LEAD[0]).wait_recv()
            start(i + LEAD[0], 0)

        for stage in range(1, 4):
            t = i + LEAD[stage]

            @pl.when(jnp.logical_and(t >= 0, t < ticks))
            def _(t=t, stage=stage):
                arrive(t, stage - 1)
                start(t, stage)

    def fill(i, carry):
        advance(i - LEAD[0])
        return carry

    lax.fori_loop(0, LEAD[0] + LAG, fill, 0)

    x_in[0].wait_recv()
    x_out[4].start()
    x_in[1].wait_recv()
    x_in[4].wait_recv()
    load_w.wait()

    def tick(place, t, carry):
        advance(t + LAG)
        arrive(t, 3)

        def one(owner, c):
            dx_part(t, place(t), owner)
            return c

        lax.fori_loop(0, 4, one, 0)
        dw_part(t, place(t))
        return carry

    def paired_tick(t, carry):
        advance(t + LAG)
        arrive(t, 3)
        wp_copy(t - BEFORE).wait_recv()
        dwp_part(t)

        def one(owner, c):
            dxp_part(t, owner)
            dx_part(t, mine(t), owner)
            return c

        lax.fori_loop(0, 4, one, 0)
        dw_part(t, mine(t))
        return carry

    lax.fori_loop(0, BEFORE, functools.partial(tick, early), 0)

    for k in (2, 3):
        x_in[k].wait_recv()
        x_out[k + 3].start()
    x_in[5].wait_recv()
    x_in[6].wait_recv()

    lax.fori_loop(BEFORE, after, paired_tick, 0)

    give = []
    for k, s in enumerate((1 - side, side)):
        copy = remote(accp.at[s * 2 + 1 - core], from_core_p.at[k], r_send.at[k], r_recv.at[k], core_dev)
        copy.start()
        give.append(copy)
    for k, (s, dev) in enumerate(((1 - side, diag_dev), (side, far_dev))):
        give[k].wait_recv()
        to_chips[k] = (accp[s * 2 + core] + from_core_p[k]).astype(jnp.bfloat16)
        copy = remote(to_chips.at[k], from_chips.at[k], r_send.at[2 + k], r_recv.at[2 + k], dev)
        copy.start()
        give.append(copy)

    last = ticks - 1
    lax.fori_loop(after, last, functools.partial(tick, late), 0)

    advance(last + LAG)
    arrive(last, 3)

    def owner_of(s, c):
        return s * 2 + c

    for k, s in enumerate((1 - side, side)):
        j = owner_of(s, 1 - core)
        dx_part(last, late(last), j)
        copy = remote(acc.at[j], from_core.at[k], r_send.at[4 + k], r_recv.at[4 + k], core_dev)
        copy.start()
        give.append(copy)
    dx_part(last, late(last), owner_of(1 - side, core))
    give[4].wait_recv()
    to_chips[2] = (acc[owner_of(1 - side, core)] + from_core[0]).astype(jnp.bfloat16)
    across = remote(to_chips.at[2], from_chips.at[2], r_send.at[6], r_recv.at[6], side_dev)
    across.start()
    give.append(across)
    dx_part(last, late(last), owner_of(side, core))
    dw_part(last, late(last))
    give[5].wait_recv()
    give[2].wait_recv()
    give[3].wait_recv()
    total = acc[owner_of(side, core)] + from_core[1]
    total += from_chips[0].astype(jnp.float32) + from_chips[1].astype(jnp.float32)
    across.wait_recv()
    dx_ref[...] = (total + from_chips[2].astype(jnp.float32)).astype(jnp.bfloat16)

    def finish(t, carry):
        far_in(t).wait_send()
        for stage in range(4):
            sent(t, stage)
        return carry

    def stored(place, t, carry):
        dw_store(t, place(t)).wait()
        return carry

    def exchanged(t, carry):
        wp_copy(t - BEFORE).wait_send()
        dwp_copy(t, theirs(t)).wait()
        return carry

    lax.fori_loop(0, ticks, finish, 0)
    lax.fori_loop(0, BEFORE, functools.partial(stored, early), 0)
    lax.fori_loop(BEFORE, after, functools.partial(stored, mine), 0)
    lax.fori_loop(after, ticks, functools.partial(stored, late), 0)
    lax.fori_loop(BEFORE, after, exchanged, 0)
    for copy in x_out:
        copy.wait_send()
    for copy in give:
        copy.wait_send()


def local(inputs, weight_in, saved_pre, grad_hidden):
    rows, model = inputs.shape
    tokens, hidden = saved_pre.shape
    pair = 2 * WIDTH
    ticks = hidden // pair - PAIRED
    vmem = pl.BlockSpec(memory_space=pltpu.VMEM)
    hbm = pl.BlockSpec(memory_space=pl.ANY)
    dma = pltpu.SemaphoreType.DMA
    return pl.pallas_call(
        functools.partial(kernel, ticks),
        out_shape=(
            jax.ShapeDtypeStruct((rows, model), jnp.bfloat16),
            jax.ShapeDtypeStruct((model, hidden), jnp.bfloat16),
        ),
        in_specs=[vmem, vmem, vmem, hbm],
        out_specs=(vmem, hbm),
        scratch_shapes=[
            pltpu.VMEM((ticks, 2, 4, 2, 4, tokens, WIDTH), jnp.bfloat16),
            pltpu.VMEM((PAIRED, 2, tokens, WIDTH), jnp.bfloat16),
            pltpu.VMEM((model, hidden), jnp.bfloat16),
            pltpu.VMEM((PAIRED, model, pair), jnp.bfloat16),
            pltpu.VMEM((model, 4 * rows), jnp.bfloat16),
            pltpu.VMEM((model, 4 * rows), jnp.bfloat16),
            pltpu.VMEM((4, rows, model), jnp.float32),
            pltpu.VMEM((4, rows, model), jnp.float32),
            pltpu.VMEM((ticks, model, pair), jnp.bfloat16),
            pltpu.VMEM((PAIRED, model, pair), jnp.bfloat16),
            pltpu.VMEM((2, rows, model), jnp.float32),
            pltpu.VMEM((2, rows, model), jnp.float32),
            pltpu.VMEM((3, rows, model), jnp.bfloat16),
            pltpu.VMEM((3, rows, model), jnp.bfloat16),
            dma((ticks, 4, 2, 2)),
            dma((ticks, 4, 2, 2)),
            dma((ticks,)),
            dma((ticks,)),
            dma((7,)),
            dma((7,)),
            dma((7,)),
            dma((7,)),
            dma((PAIRED,)),
            dma((PAIRED,)),
            dma((PAIRED,)),
            dma((PAIRED,)),
            dma,
            dma((ticks,)),
        ],
        compiler_params=pltpu.CompilerParams(
            collective_id=0, has_side_effects=True, vmem_limit_bytes=60 * 2**20
        ),
        name="gather_and_multiply",
    )(inputs, saved_pre, grad_hidden, weight_in)


def solution(mesh):
    return jax.shard_map(
        local,
        mesh=mesh,
        in_specs=(
            P("col", ("row", "depth")),
            P(("row", "depth"), "col"),
            P(("row", "depth"), "col"),
            P(("row", "depth"), "col"),
        ),
        out_specs=(P("col", ("row", "depth")), P(("row", "depth"), "col")),
        check_vma=False,
    )
```

```python
import functools

import jax
import jax.numpy as jnp
from jax import lax
from jax.experimental import pallas as pl
from jax.experimental.pallas import tpu as pltpu
from jax.sharding import PartitionSpec as P

MESH = pl.DeviceIdType.MESH
WIDTH = 256
LEAD = (3, 2, 1, 0)
LAG = 1
PAIRED = 3
BEFORE = 1
ROOT = 0.7978845608028654
CUBE = 0.044715


def gelu_back(grad_hidden, saved_pre):
    a = saved_pre.astype(jnp.float32)
    square = a * a
    t = jnp.tanh(ROOT * (a + CUBE * (square * a)))
    slope = 0.5 * (1.0 + t) + 0.5 * a * (1.0 - t * t) * (ROOT * (1.0 + (3.0 * CUBE) * square))
    return (grad_hidden.astype(jnp.float32) * slope).astype(jnp.bfloat16)


def kernel(ticks, x_ref, pre_ref, gh_ref, w_hbm, dx_ref, dw_ref, gall, gout, wv, wp, xt, xtp, acc, accp, dwp,
           from_core, from_core_p, to_chips, from_chips, g_send, g_recv, p_send, p_recv, x_send, x_recv, r_send, r_recv,
           wp_send, wp_recv, dwp_send, dwp_recv, w_sem):
    y = lax.axis_index("row")
    col = lax.axis_index("col")
    depth = lax.axis_index("depth")
    side, core = col // 2, col % 2
    far, z = depth // 4, depth % 4
    y_up, y_down = (y + 1) % 4, (y + 3) % 4
    z_up, z_down = (z + 1) % 4, (z + 3) % 4
    y_dev = ((y_up, col, depth), (y_down, col, depth))
    z_dev = ((y, col, far * 4 + z_up), (y, col, far * 4 + z_down))
    far_dev = (y, col, (1 - far) * 4 + z)
    side_dev = (y, (1 - side) * 2 + core, depth)
    core_dev = (y, side * 2 + 1 - core, depth)
    diag_dev = (y, (1 - side) * 2 + core, (1 - far) * 4 + z)
    rows, model = x_ref.shape
    pair = 2 * WIDTH

    load_w = pltpu.make_async_copy(w_hbm, wv, w_sem)
    load_w.start()

    barrier = pltpu.get_barrier_semaphore()
    for dev in (*y_dev, *z_dev, far_dev, side_dev, core_dev, diag_dev):
        pl.semaphore_signal(barrier, 1, device_id=dev, device_id_type=MESH)

    def remote(src, dst, send, recv, dev):
        return pltpu.make_async_remote_copy(src, dst, send, recv, device_id=dev, device_id_type=MESH)

    def far_in(t):
        place = gall.at[t, :, y, 1 - far, z]
        return remote(place, place, p_send.at[t], p_recv.at[t], far_dev)

    def early(t):
        return pl.multiple_of(t * pair, pair)

    def mine(t):
        return pl.multiple_of((t + far * PAIRED) * pair, pair)

    def theirs(t):
        return pl.multiple_of((t + (1 - far) * PAIRED) * pair, pair)

    def late(t):
        return pl.multiple_of((t + PAIRED) * pair, pair)

    def places(t, stage, chunk, way):
        up = way == 0
        if chunk == 0:
            first_in, first_out = (y_down, y_up) if up else (y_up, y_down)
            second_in = z_down if up else z_up
            if stage in (0, 4):
                half = far if stage == 4 else 1 - far
                return gall.at[t, 0, y, half, z], gall.at[t, 0, first_in, half, z], y_dev[way]
            if stage == 1:
                return gall.at[t, 0, first_in, way, z], gall.at[t, 0, (y + 2) % 4, way, z], y_dev[way]
            if stage == 2:
                return gall.at[t, 0, :, :, z], gall.at[t, 0, :, :, second_in], z_dev[way]
            return gall.at[t, 0, :, way, second_in], gall.at[t, 0, :, way, (z + 2) % 4], z_dev[way]
        first_in = z_down if up else z_up
        second_in = y_down if up else y_up
        if stage in (0, 4):
            half = far if stage == 4 else 1 - far
            return gall.at[t, 1, y, half, z], gall.at[t, 1, y, half, first_in], z_dev[way]
        if stage == 1:
            return gall.at[t, 1, y, way, first_in], gall.at[t, 1, y, way, (z + 2) % 4], z_dev[way]
        if stage == 2:
            return gall.at[t, 1, y], gall.at[t, 1, second_in], y_dev[way]
        return gall.at[t, 1, second_in, way], gall.at[t, 1, (y + 2) % 4, way], y_dev[way]

    def start(t, stage):
        for chunk in range(2):
            for way in range(2):
                out, _, dev = places(t, stage, chunk, way)
                remote(out, out, g_send.at[t, stage, chunk, way], g_recv.at[t, stage, chunk, way], dev).start()

    def arrive(t, stage):
        for chunk in range(2):
            for way in range(2):
                _, come, dev = places(t, stage, chunk, way)
                remote(come, come, g_send.at[t, stage, chunk, way], g_recv.at[t, stage, chunk, way], dev).wait_recv()

    def sent(t, stage):
        for chunk in range(2):
            for way in range(2):
                out, _, dev = places(t, stage, chunk, way)
                remote(out, out, g_send.at[t, stage, chunk, way], g_recv.at[t, stage, chunk, way], dev).wait_send()

    def grad_at(base, chunk):
        cols = pl.ds(pl.multiple_of(base + chunk * WIDTH, WIDTH), WIDTH)
        return gelu_back(gh_ref[:, cols], pre_ref[:, cols])

    def own_grad(place, t, carry):
        for chunk in range(2):
            gall[t, chunk, y, far, z] = grad_at(place(t), chunk)
        return carry

    def paired_grad(t, carry):
        for chunk in range(2):
            gout[t - BEFORE, chunk] = grad_at(theirs(t), chunk)
            gall[t, chunk, y, far, z] = grad_at(mine(t), chunk)
        return carry

    after = BEFORE + PAIRED
    lax.fori_loop(0, BEFORE, functools.partial(own_grad, early), 0)
    lax.fori_loop(BEFORE, after, paired_grad, 0)
    lax.fori_loop(after, ticks, functools.partial(own_grad, late), 0)
    own = pl.ds(pl.multiple_of(col * rows, rows), rows)
    xt[:, own] = x_ref[...].T
    pl.semaphore_wait(barrier, 8)

    def own_out(t, carry):
        out = gall.at[t, :, y, far, z]
        remote(out, out, p_send.at[t], p_recv.at[t], far_dev).start()
        start(t, 4)
        return carry

    def paired_out(t, carry):
        remote(gout.at[t - BEFORE], gall.at[t, :, y, far, z], p_send.at[t], p_recv.at[t], far_dev).start()
        start(t, 4)
        return carry

    lax.fori_loop(0, BEFORE, own_out, 0)
    lax.fori_loop(BEFORE, after, paired_out, 0)

    own = pl.ds(pl.multiple_of(col * rows, rows), rows)
    beside = pl.ds(pl.multiple_of(((1 - side) * 2 + core) * rows, rows), rows)
    near = pl.ds(pl.multiple_of((side * 2 + 1 - core) * rows, rows), rows)
    cross = pl.ds(pl.multiple_of(((1 - side) * 2 + 1 - core) * rows, rows), rows)

    def x_copy(k, src, dst, dev):
        return remote(src, dst, x_send.at[k], x_recv.at[k], dev)

    low, high = pl.ds(0, model // 2), pl.ds(model // 2, model // 2)
    x_out = [
        x_copy(0, xt.at[:, own], xt.at[:, own], side_dev),
        x_copy(1, xt.at[:, own], xtp.at[:, own], diag_dev),
        x_copy(2, xt.at[:, own], xt.at[:, own], core_dev),
        x_copy(3, xt.at[low, own], xtp.at[low, own], far_dev),
        x_copy(4, xt.at[high, own], xtp.at[high, own], far_dev),
        x_copy(5, xt.at[:, beside], xt.at[:, beside], core_dev),
        x_copy(6, xtp.at[:, beside], xtp.at[:, beside], core_dev),
        x_copy(7, xtp.at[:, own], xtp.at[:, own], core_dev),
    ]
    x_in = [
        x_copy(0, xt.at[:, beside], xt.at[:, beside], side_dev),
        x_copy(1, xtp.at[:, beside], xtp.at[:, beside], diag_dev),
        x_copy(2, xt.at[:, near], xt.at[:, near], core_dev),
        x_copy(3, xtp.at[low, own], xtp.at[low, own], diag_dev),
        x_copy(4, xtp.at[high, own], xtp.at[high, own], side_dev),
        x_copy(5, xt.at[:, cross], xt.at[:, cross], core_dev),
        x_copy(6, xtp.at[:, cross], xtp.at[:, cross], core_dev),
        x_copy(7, xtp.at[:, near], xtp.at[:, near], core_dev),
    ]
    for copy in x_out[:5]:
        copy.start()
    lax.fori_loop(after, ticks, own_out, 0)

    def wp_copy(k):
        return remote(
            w_hbm.at[:, pl.ds(theirs(k + BEFORE), pair)], wp.at[k], wp_send.at[k], wp_recv.at[k], far_dev
        )

    def send_weights(k, carry):
        wp_copy(k).start()
        return carry

    lax.fori_loop(0, PAIRED, send_weights, 0)

    accp[...] = jnp.zeros_like(accp)
    acc[...] = jnp.zeros_like(acc)

    def dx_part(t, base, owner):
        total = acc[owner]
        for chunk in range(2):
            cols = pl.ds(pl.multiple_of(base + chunk * WIDTH, WIDTH), WIDTH)
            g = gall[t, chunk, owner].reshape(rows, WIDTH)
            total += lax.dot_general(g, wv[:, cols], (((1,), (1,)), ((), ())), preferred_element_type=jnp.float32)
        acc[owner] = total

    def dxp_part(t, owner):
        total = accp[owner]
        for chunk in range(2):
            w = wp[t - BEFORE, :, pl.ds(chunk * WIDTH, WIDTH)]
            g = gall[t, chunk, owner].reshape(rows, WIDTH)
            total += lax.dot_general(g, w, (((1,), (1,)), ((), ())), preferred_element_type=jnp.float32)
        accp[owner] = total

    def dw_part(t, base):
        for chunk in range(2):
            g = gall[t, chunk].reshape(4 * rows, WIDTH)
            cols = pl.ds(pl.multiple_of(base + chunk * WIDTH, WIDTH), WIDTH)
            dw_ref[:, cols] = jnp.dot(
                xt[...], g, preferred_element_type=jnp.float32
            ).astype(jnp.bfloat16)

    def dwp_copy(t, base):
        k = t - BEFORE
        return remote(dwp.at[k], dw_ref.at[:, pl.ds(base, pair)], dwp_send.at[k], dwp_recv.at[k], far_dev)

    def dwp_part(t):
        for chunk in range(2):
            g = gall[t, chunk].reshape(4 * rows, WIDTH)
            dwp[t - BEFORE, :, pl.ds(chunk * WIDTH, WIDTH)] = jnp.dot(
                xtp[...], g, preferred_element_type=jnp.float32
            ).astype(jnp.bfloat16)
        dwp_copy(t, mine(t)).start()

    def advance(i):
        @pl.when(i + LEAD[0] < ticks)
        def _():
            far_in(i + LEAD[0]).wait_recv()
            start(i + LEAD[0], 0)

        for stage in range(1, 4):
            t = i + LEAD[stage]

            @pl.when(jnp.logical_and(t >= 0, t < ticks))
            def _(t=t, stage=stage):
                if stage == 1:
                    arrive(t, 4)
                arrive(t, stage - 1)
                start(t, stage)

    def fill(i, carry):
        advance(i - LEAD[0])
        return carry

    lax.fori_loop(0, LEAD[0] + LAG, fill, 0)

    x_in[0].wait_recv()
    x_out[5].start()
    x_in[1].wait_recv()
    x_out[6].start()
    x_in[2].wait_recv()
    x_in[5].wait_recv()
    load_w.wait()

    def tick(place, t, carry):
        advance(t + LAG)
        arrive(t, 3)

        def one(owner, c):
            dx_part(t, place(t), owner)
            return c

        lax.fori_loop(0, 4, one, 0)
        dw_part(t, place(t))
        return carry

    def paired_tick(t, carry):
        advance(t + LAG)
        arrive(t, 3)
        wp_copy(t - BEFORE).wait_recv()
        dwp_part(t)

        def one(owner, c):
            dxp_part(t, owner)
            dx_part(t, mine(t), owner)
            return c

        lax.fori_loop(0, 4, one, 0)
        dw_part(t, mine(t))
        return carry

    lax.fori_loop(0, BEFORE, functools.partial(tick, early), 0)

    x_in[3].wait_recv()
    x_in[4].wait_recv()
    x_out[7].start()
    x_in[6].wait_recv()
    x_in[7].wait_recv()

    lax.fori_loop(BEFORE, after, paired_tick, 0)

    give = []
    for k, s in enumerate((side, 1 - side)):
        copy = remote(accp.at[s * 2 + 1 - core], from_core_p.at[k], r_send.at[k], r_recv.at[k], core_dev)
        copy.start()
        give.append(copy)
    for k, s in enumerate((side, 1 - side)):
        give[k].wait_recv()
        to_chips[k] = (accp[s * 2 + core] + from_core_p[k]).astype(jnp.bfloat16)
        copy = remote(to_chips.at[k], from_chips.at[k], r_send.at[2 + k], r_recv.at[2 + k], diag_dev)
        copy.start()
        give.append(copy)

    last = ticks - 1
    lax.fori_loop(after, last, functools.partial(tick, late), 0)

    advance(last + LAG)
    arrive(last, 3)

    half = rows // 2

    def dx_half(owner, h):
        total = acc[owner, h * half : (h + 1) * half]
        for chunk in range(2):
            cols = pl.ds(pl.multiple_of(late(last) + chunk * WIDTH, WIDTH), WIDTH)
            g = gall[last, chunk, owner, h].reshape(half, WIDTH)
            total += lax.dot_general(g, wv[:, cols], (((1,), (1,)), ((), ())), preferred_element_type=jnp.float32)
        return total

    def part(h):
        return pl.ds(h * half, half)

    def exchange(k, src, dst, dev):
        copy = remote(src, dst, r_send.at[k], r_recv.at[k], dev)
        copy.start()
        give.append(copy)
        return copy

    to_core = []
    for h in range(2):
        j = (1 - side) * 2 + 1 - core
        acc[j, h * half : (h + 1) * half] = dx_half(j, h)
        to_core.append(exchange(4 + h, acc.at[j, part(h)], from_core.at[0, part(h)], core_dev))
    across = []
    for h in range(2):
        total = dx_half((1 - side) * 2 + core, h)
        to_core[h].wait_recv()
        if h == 0:
            give[2].wait_recv()
        total += from_core[0, h * half : (h + 1) * half]
        total += from_chips[0, h * half : (h + 1) * half].astype(jnp.float32)
        to_chips[2, h * half : (h + 1) * half] = total.astype(jnp.bfloat16)
        across.append(exchange(6 + h, to_chips.at[2, part(h)], from_chips.at[2, part(h)], side_dev))
    for h in range(2):
        j = side * 2 + 1 - core
        acc[j, h * half : (h + 1) * half] = dx_half(j, h)
        to_core.append(exchange(8 + h, acc.at[j, part(h)], from_core.at[1, part(h)], core_dev))
    dw_part(last, late(last))
    for h in range(2):
        j = side * 2 + core
        total = dx_half(j, h)
        to_core[2 + h].wait_recv()
        acc[j, h * half : (h + 1) * half] = total + from_core[1, h * half : (h + 1) * half]
    for h in range(2):
        total = acc[side * 2 + core, h * half : (h + 1) * half]
        if h == 0:
            give[3].wait_recv()
        total += from_chips[1, h * half : (h + 1) * half].astype(jnp.float32)
        across[h].wait_recv()
        other = from_chips[2, h * half : (h + 1) * half].astype(jnp.float32)
        dx_ref[h * half : (h + 1) * half, :] = (total + other).astype(jnp.bfloat16)

    def finish(t, carry):
        far_in(t).wait_send()
        for stage in range(5):
            sent(t, stage)
        return carry

    def exchanged(t, carry):
        wp_copy(t - BEFORE).wait_send()
        dwp_copy(t, theirs(t)).wait()
        return carry

    lax.fori_loop(0, ticks, finish, 0)
    lax.fori_loop(BEFORE, after, exchanged, 0)
    for copy in x_out:
        copy.wait_send()
    for copy in give:
        copy.wait_send()


def local(inputs, weight_in, saved_pre, grad_hidden):
    rows, model = inputs.shape
    tokens, hidden = saved_pre.shape
    pair = 2 * WIDTH
    ticks = hidden // pair - PAIRED
    vmem = pl.BlockSpec(memory_space=pltpu.VMEM)
    hbm = pl.BlockSpec(memory_space=pl.ANY)
    dma = pltpu.SemaphoreType.DMA
    return pl.pallas_call(
        functools.partial(kernel, ticks),
        out_shape=(
            jax.ShapeDtypeStruct((rows, model), jnp.bfloat16),
            pltpu.VMEM((model, hidden), jnp.bfloat16),
        ),
        in_specs=[vmem, vmem, vmem, hbm],
        out_specs=(vmem, vmem),
        scratch_shapes=[
            pltpu.VMEM((ticks, 2, 4, 2, 4, tokens, WIDTH), jnp.bfloat16),
            pltpu.VMEM((PAIRED, 2, tokens, WIDTH), jnp.bfloat16),
            pltpu.VMEM((model, hidden), jnp.bfloat16),
            pltpu.VMEM((PAIRED, model, pair), jnp.bfloat16),
            pltpu.VMEM((model, 4 * rows), jnp.bfloat16),
            pltpu.VMEM((model, 4 * rows), jnp.bfloat16),
            pltpu.VMEM((4, rows, model), jnp.float32),
            pltpu.VMEM((4, rows, model), jnp.float32),
            pltpu.VMEM((PAIRED, model, pair), jnp.bfloat16),
            pltpu.VMEM((2, rows, model), jnp.float32),
            pltpu.VMEM((2, rows, model), jnp.float32),
            pltpu.VMEM((3, rows, model), jnp.bfloat16),
            pltpu.VMEM((3, rows, model), jnp.bfloat16),
            dma((ticks, 5, 2, 2)),
            dma((ticks, 5, 2, 2)),
            dma((ticks,)),
            dma((ticks,)),
            dma((8,)),
            dma((8,)),
            dma((11,)),
            dma((11,)),
            dma((PAIRED,)),
            dma((PAIRED,)),
            dma((PAIRED,)),
            dma((PAIRED,)),
            dma,
        ],
        compiler_params=pltpu.CompilerParams(
            collective_id=0, has_side_effects=True, vmem_limit_bytes=48 * 2**20
        ),
        name="gather_and_multiply",
    )(inputs, saved_pre, grad_hidden, weight_in)


def solution(mesh):
    return jax.shard_map(
        local,
        mesh=mesh,
        in_specs=(
            P("col", ("row", "depth")),
            P(("row", "depth"), "col"),
            P(("row", "depth"), "col"),
            P(("row", "depth"), "col"),
        ),
        out_specs=(P("col", ("row", "depth")), P(("row", "depth"), "col")),
        check_vma=False,
    )
```

```python
import functools

import jax
import jax.numpy as jnp
from jax import lax
from jax.experimental import pallas as pl
from jax.experimental.pallas import tpu as pltpu
from jax.sharding import PartitionSpec as P

MESH = pl.DeviceIdType.MESH
WIDTH = 256
LEAD = (3, 2, 1, 0)
LAG = 1
PAIRED = 4
BEFORE = 1
ROOT = 0.7978845608028654
CUBE = 0.044715


def gelu_back(grad_hidden, saved_pre):
    a = saved_pre.astype(jnp.float32)
    square = a * a
    t = jnp.tanh(ROOT * (a + CUBE * (square * a)))
    slope = 0.5 * (1.0 + t) + 0.5 * a * (1.0 - t * t) * (ROOT * (1.0 + (3.0 * CUBE) * square))
    return (grad_hidden.astype(jnp.float32) * slope).astype(jnp.bfloat16)


def kernel(ticks, x_hbm, pre_hbm, gh_hbm, w_hbm, dx_ref, dw_ref, gall, gout, wv, wp, xt, xtp, acc, accp, dwp,
           x_ref, pre_ref, gh_ref, from_core, from_core_p, to_chips, from_chips, g_send, g_recv, p_send, p_recv, x_send, x_recv, r_send, r_recv,
           wp_send, wp_recv, dwp_send, dwp_recv, w_sem, in_sem):
    y = lax.axis_index("row")
    col = lax.axis_index("col")
    depth = lax.axis_index("depth")
    side, core = col // 2, col % 2
    far, z = depth // 4, depth % 4
    y_up, y_down = (y + 1) % 4, (y + 3) % 4
    z_up, z_down = (z + 1) % 4, (z + 3) % 4
    y_dev = ((y_up, col, depth), (y_down, col, depth))
    z_dev = ((y, col, far * 4 + z_up), (y, col, far * 4 + z_down))
    far_dev = (y, col, (1 - far) * 4 + z)
    side_dev = (y, (1 - side) * 2 + core, depth)
    core_dev = (y, side * 2 + 1 - core, depth)
    diag_dev = (y, (1 - side) * 2 + core, (1 - far) * 4 + z)
    rows, model = x_ref.shape
    pair = 2 * WIDTH

    load_w = pltpu.make_async_copy(w_hbm, wv, w_sem)
    loads = [
        pltpu.make_async_copy(src, dst, in_sem.at[k])
        for k, (src, dst) in enumerate(((pre_hbm, pre_ref), (gh_hbm, gh_ref), (x_hbm, x_ref)))
    ]
    for copy in loads:
        copy.start()
    load_w.start()

    barrier = pltpu.get_barrier_semaphore()
    for dev in (*y_dev, *z_dev, far_dev, side_dev, core_dev, diag_dev):
        pl.semaphore_signal(barrier, 1, device_id=dev, device_id_type=MESH)

    def remote(src, dst, send, recv, dev):
        return pltpu.make_async_remote_copy(src, dst, send, recv, device_id=dev, device_id_type=MESH)

    def far_in(t):
        place = gall.at[t, :, y, 1 - far, z]
        return remote(place, place, p_send.at[t], p_recv.at[t], far_dev)

    def early(t):
        return pl.multiple_of(t * pair, pair)

    def mine(t):
        return pl.multiple_of((t + far * PAIRED) * pair, pair)

    def theirs(t):
        return pl.multiple_of((t + (1 - far) * PAIRED) * pair, pair)

    def late(t):
        return pl.multiple_of((t + PAIRED) * pair, pair)

    def places(t, stage, chunk, way):
        up = way == 0
        if chunk == 0:
            first_in, first_out = (y_down, y_up) if up else (y_up, y_down)
            second_in = z_down if up else z_up
            if stage in (0, 4):
                half = far if stage == 4 else 1 - far
                return gall.at[t, 0, y, half, z], gall.at[t, 0, first_in, half, z], y_dev[way]
            if stage == 1:
                return gall.at[t, 0, first_in, way, z], gall.at[t, 0, (y + 2) % 4, way, z], y_dev[way]
            if stage == 2:
                return gall.at[t, 0, :, :, z], gall.at[t, 0, :, :, second_in], z_dev[way]
            return gall.at[t, 0, :, way, second_in], gall.at[t, 0, :, way, (z + 2) % 4], z_dev[way]
        first_in = z_down if up else z_up
        second_in = y_down if up else y_up
        if stage in (0, 4):
            half = far if stage == 4 else 1 - far
            return gall.at[t, 1, y, half, z], gall.at[t, 1, y, half, first_in], z_dev[way]
        if stage == 1:
            return gall.at[t, 1, y, way, first_in], gall.at[t, 1, y, way, (z + 2) % 4], z_dev[way]
        if stage == 2:
            return gall.at[t, 1, y], gall.at[t, 1, second_in], y_dev[way]
        return gall.at[t, 1, second_in, way], gall.at[t, 1, (y + 2) % 4, way], y_dev[way]

    def start(t, stage):
        for chunk in range(2):
            for way in range(2):
                out, _, dev = places(t, stage, chunk, way)
                remote(out, out, g_send.at[t, stage, chunk, way], g_recv.at[t, stage, chunk, way], dev).start()

    def arrive(t, stage):
        for chunk in range(2):
            for way in range(2):
                _, come, dev = places(t, stage, chunk, way)
                remote(come, come, g_send.at[t, stage, chunk, way], g_recv.at[t, stage, chunk, way], dev).wait_recv()

    def sent(t, stage):
        for chunk in range(2):
            for way in range(2):
                out, _, dev = places(t, stage, chunk, way)
                remote(out, out, g_send.at[t, stage, chunk, way], g_recv.at[t, stage, chunk, way], dev).wait_send()

    def grad_at(base, chunk):
        cols = pl.ds(pl.multiple_of(base + chunk * WIDTH, WIDTH), WIDTH)
        return gelu_back(gh_ref[:, cols], pre_ref[:, cols])

    def own_grad(place, t, carry):
        for chunk in range(2):
            gall[t, chunk, y, far, z] = grad_at(place(t), chunk)
        return carry

    def paired_grad(t, carry):
        for chunk in range(2):
            gout[t - BEFORE, chunk] = grad_at(theirs(t), chunk)
            gall[t, chunk, y, far, z] = grad_at(mine(t), chunk)
        return carry

    after = BEFORE + PAIRED
    loads[0].wait()
    loads[1].wait()
    lax.fori_loop(0, BEFORE, functools.partial(own_grad, early), 0)
    lax.fori_loop(BEFORE, after, paired_grad, 0)
    lax.fori_loop(after, ticks, functools.partial(own_grad, late), 0)
    own = pl.ds(pl.multiple_of(col * rows, rows), rows)
    loads[2].wait()
    xt[:, own] = x_ref[...].T
    pl.semaphore_wait(barrier, 8)

    def own_out(t, carry):
        out = gall.at[t, :, y, far, z]
        remote(out, out, p_send.at[t], p_recv.at[t], far_dev).start()
        start(t, 4)
        return carry

    def paired_out(t, carry):
        remote(gout.at[t - BEFORE], gall.at[t, :, y, far, z], p_send.at[t], p_recv.at[t], far_dev).start()
        start(t, 4)
        return carry

    lax.fori_loop(0, BEFORE, own_out, 0)
    lax.fori_loop(BEFORE, after, paired_out, 0)

    own = pl.ds(pl.multiple_of(col * rows, rows), rows)
    beside = pl.ds(pl.multiple_of(((1 - side) * 2 + core) * rows, rows), rows)
    near = pl.ds(pl.multiple_of((side * 2 + 1 - core) * rows, rows), rows)
    cross = pl.ds(pl.multiple_of(((1 - side) * 2 + 1 - core) * rows, rows), rows)

    def x_copy(k, src, dst, dev):
        return remote(src, dst, x_send.at[k], x_recv.at[k], dev)

    low, high = pl.ds(0, model // 2), pl.ds(model // 2, model // 2)
    x_out = [
        x_copy(0, xt.at[:, own], xt.at[:, own], side_dev),
        x_copy(1, xt.at[:, own], xtp.at[:, own], diag_dev),
        x_copy(2, xt.at[:, own], xt.at[:, own], core_dev),
        x_copy(3, xt.at[low, beside], xtp.at[low, beside], diag_dev),
        x_copy(4, xtp.at[high, beside], xtp.at[high, beside], side_dev),
        x_copy(5, xt.at[:, beside], xt.at[:, beside], core_dev),
        x_copy(6, xtp.at[:, beside], xtp.at[:, beside], core_dev),
        x_copy(7, xtp.at[:, own], xtp.at[:, own], core_dev),
    ]
    x_in = [
        x_copy(0, xt.at[:, beside], xt.at[:, beside], side_dev),
        x_copy(1, xtp.at[:, beside], xtp.at[:, beside], diag_dev),
        x_copy(2, xt.at[:, near], xt.at[:, near], core_dev),
        x_copy(3, xtp.at[low, own], xtp.at[low, own], diag_dev),
        x_copy(4, xtp.at[high, own], xtp.at[high, own], side_dev),
        x_copy(5, xt.at[:, cross], xt.at[:, cross], core_dev),
        x_copy(6, xtp.at[:, cross], xtp.at[:, cross], core_dev),
        x_copy(7, xtp.at[:, near], xtp.at[:, near], core_dev),
    ]
    for copy in x_out[:3]:
        copy.start()
    lax.fori_loop(after, ticks, own_out, 0)

    def wp_copy(k):
        return remote(
            w_hbm.at[:, pl.ds(theirs(k + BEFORE), pair)], wp.at[k], wp_send.at[k], wp_recv.at[k], far_dev
        )

    def send_weights(k, carry):
        wp_copy(k).start()
        return carry

    lax.fori_loop(0, 1, send_weights, 0)

    accp[...] = jnp.zeros_like(accp)
    acc[...] = jnp.zeros_like(acc)

    def dx_part(t, base, owner):
        total = acc[owner]
        for chunk in range(2):
            cols = pl.ds(pl.multiple_of(base + chunk * WIDTH, WIDTH), WIDTH)
            g = gall[t, chunk, owner].reshape(rows, WIDTH)
            total += lax.dot_general(g, wv[:, cols], (((1,), (1,)), ((), ())), preferred_element_type=jnp.float32)
        acc[owner] = total

    def dxp_part(t, owner):
        total = accp[owner]
        for chunk in range(2):
            w = wp[t - BEFORE, :, pl.ds(chunk * WIDTH, WIDTH)]
            g = gall[t, chunk, owner].reshape(rows, WIDTH)
            total += lax.dot_general(g, w, (((1,), (1,)), ((), ())), preferred_element_type=jnp.float32)
        accp[owner] = total

    def dw_part(t, base):
        for chunk in range(2):
            g = gall[t, chunk].reshape(4 * rows, WIDTH)
            cols = pl.ds(pl.multiple_of(base + chunk * WIDTH, WIDTH), WIDTH)
            dw_ref[:, cols] = jnp.dot(
                xt[...], g, preferred_element_type=jnp.float32
            ).astype(jnp.bfloat16)

    def dwp_copy(t, base):
        k = t - BEFORE
        return remote(dwp.at[k], dw_ref.at[:, pl.ds(base, pair)], dwp_send.at[k], dwp_recv.at[k], far_dev)

    def dwp_part(t):
        for chunk in range(2):
            g = gall[t, chunk].reshape(4 * rows, WIDTH)
            dwp[t - BEFORE, :, pl.ds(chunk * WIDTH, WIDTH)] = jnp.dot(
                xtp[...], g, preferred_element_type=jnp.float32
            ).astype(jnp.bfloat16)
        dwp_copy(t, mine(t)).start()

    def advance(i):
        @pl.when(i + LEAD[0] < ticks)
        def _():
            far_in(i + LEAD[0]).wait_recv()
            start(i + LEAD[0], 0)

        for stage in range(1, 4):
            t = i + LEAD[stage]

            @pl.when(jnp.logical_and(t >= 0, t < ticks))
            def _(t=t, stage=stage):
                if stage == 1:
                    arrive(t, 4)
                arrive(t, stage - 1)
                start(t, stage)

    def fill(i, carry):
        advance(i - LEAD[0])
        return carry

    lax.fori_loop(0, LEAD[0] + LAG, fill, 0)

    x_in[0].wait_recv()
    x_out[3].start()
    x_in[1].wait_recv()
    x_out[4].start()
    lax.fori_loop(1, PAIRED, send_weights, 0)
    x_out[5].start()
    x_out[6].start()
    x_in[2].wait_recv()
    x_in[5].wait_recv()
    load_w.wait()

    def tick(place, t, carry):
        advance(t + LAG)
        arrive(t, 3)

        def one(owner, c):
            dx_part(t, place(t), owner)
            return c

        lax.fori_loop(0, 4, one, 0)
        dw_part(t, place(t))
        return carry

    def paired_tick(t, carry):
        advance(t + LAG)
        arrive(t, 3)
        wp_copy(t - BEFORE).wait_recv()
        dwp_part(t)

        def one(owner, c):
            dxp_part(t, owner)
            dx_part(t, mine(t), owner)
            return c

        lax.fori_loop(0, 4, one, 0)
        dw_part(t, mine(t))
        return carry

    lax.fori_loop(0, BEFORE, functools.partial(tick, early), 0)

    x_in[3].wait_recv()
    x_in[4].wait_recv()
    x_out[7].start()
    x_in[6].wait_recv()
    x_in[7].wait_recv()

    lax.fori_loop(BEFORE, after, paired_tick, 0)

    give = []
    for k, s in enumerate((side, 1 - side)):
        copy = remote(accp.at[s * 2 + 1 - core], from_core_p.at[k], r_send.at[k], r_recv.at[k], core_dev)
        copy.start()
        give.append(copy)
    for k, s in enumerate((side, 1 - side)):
        give[k].wait_recv()
        to_chips[k] = (accp[s * 2 + core] + from_core_p[k]).astype(jnp.bfloat16)
        copy = remote(to_chips.at[k], from_chips.at[k], r_send.at[2 + k], r_recv.at[2 + k], diag_dev)
        copy.start()
        give.append(copy)

    last = ticks - 1
    lax.fori_loop(after, last, functools.partial(tick, late), 0)

    advance(last + LAG)
    arrive(last, 3)

    half = rows // 2

    def dx_half(owner, h):
        total = acc[owner, h * half : (h + 1) * half]
        for chunk in range(2):
            cols = pl.ds(pl.multiple_of(late(last) + chunk * WIDTH, WIDTH), WIDTH)
            g = gall[last, chunk, owner, h].reshape(half, WIDTH)
            total += lax.dot_general(g, wv[:, cols], (((1,), (1,)), ((), ())), preferred_element_type=jnp.float32)
        return total

    def part(h):
        return pl.ds(h * half, half)

    def exchange(k, src, dst, dev):
        copy = remote(src, dst, r_send.at[k], r_recv.at[k], dev)
        copy.start()
        give.append(copy)
        return copy

    to_core = []
    for h in range(2):
        j = (1 - side) * 2 + 1 - core
        acc[j, h * half : (h + 1) * half] = dx_half(j, h)
        to_core.append(exchange(4 + h, acc.at[j, part(h)], from_core.at[0, part(h)], core_dev))
    across = []
    for h in range(2):
        total = dx_half((1 - side) * 2 + core, h)
        to_core[h].wait_recv()
        if h == 0:
            give[2].wait_recv()
        total += from_core[0, h * half : (h + 1) * half]
        total += from_chips[0, h * half : (h + 1) * half].astype(jnp.float32)
        to_chips[2, h * half : (h + 1) * half] = total.astype(jnp.bfloat16)
        across.append(exchange(6 + h, to_chips.at[2, part(h)], from_chips.at[2, part(h)], side_dev))
    for h in range(2):
        j = side * 2 + 1 - core
        acc[j, h * half : (h + 1) * half] = dx_half(j, h)
        to_core.append(exchange(8 + h, acc.at[j, part(h)], from_core.at[1, part(h)], core_dev))
    dw_part(last, late(last))
    for h in range(2):
        j = side * 2 + core
        total = dx_half(j, h)
        to_core[2 + h].wait_recv()
        acc[j, h * half : (h + 1) * half] = total + from_core[1, h * half : (h + 1) * half]
    for h in range(2):
        total = acc[side * 2 + core, h * half : (h + 1) * half]
        if h == 0:
            give[3].wait_recv()
        total += from_chips[1, h * half : (h + 1) * half].astype(jnp.float32)
        across[h].wait_recv()
        other = from_chips[2, h * half : (h + 1) * half].astype(jnp.float32)
        dx_ref[h * half : (h + 1) * half, :] = (total + other).astype(jnp.bfloat16)

    def finish(t, carry):
        far_in(t).wait_send()
        for stage in range(5):
            sent(t, stage)
        return carry

    def exchanged(t, carry):
        wp_copy(t - BEFORE).wait_send()
        dwp_copy(t, theirs(t)).wait()
        return carry

    lax.fori_loop(0, ticks, finish, 0)
    lax.fori_loop(BEFORE, after, exchanged, 0)
    for copy in x_out:
        copy.wait_send()
    for copy in give:
        copy.wait_send()


def local(inputs, weight_in, saved_pre, grad_hidden):
    rows, model = inputs.shape
    tokens, hidden = saved_pre.shape
    pair = 2 * WIDTH
    ticks = hidden // pair - PAIRED
    vmem = pl.BlockSpec(memory_space=pltpu.VMEM)
    hbm = pl.BlockSpec(memory_space=pl.ANY)
    dma = pltpu.SemaphoreType.DMA
    return pl.pallas_call(
        functools.partial(kernel, ticks),
        out_shape=(
            pltpu.VMEM((rows, model), jnp.bfloat16),
            pltpu.VMEM((model, hidden), jnp.bfloat16),
        ),
        in_specs=[hbm, hbm, hbm, hbm],
        out_specs=(vmem, vmem),
        scratch_shapes=[
            pltpu.VMEM((ticks, 2, 4, 2, 4, tokens, WIDTH), jnp.bfloat16),
            pltpu.VMEM((PAIRED, 2, tokens, WIDTH), jnp.bfloat16),
            pltpu.VMEM((model, hidden), jnp.bfloat16),
            pltpu.VMEM((PAIRED, model, pair), jnp.bfloat16),
            pltpu.VMEM((model, 4 * rows), jnp.bfloat16),
            pltpu.VMEM((model, 4 * rows), jnp.bfloat16),
            pltpu.VMEM((4, rows, model), jnp.float32),
            pltpu.VMEM((4, rows, model), jnp.float32),
            pltpu.VMEM((PAIRED, model, pair), jnp.bfloat16),
            pltpu.VMEM((rows, model), jnp.bfloat16),
            pltpu.VMEM((tokens, hidden), jnp.bfloat16),
            pltpu.VMEM((tokens, hidden), jnp.bfloat16),
            pltpu.VMEM((2, rows, model), jnp.float32),
            pltpu.VMEM((2, rows, model), jnp.float32),
            pltpu.VMEM((3, rows, model), jnp.bfloat16),
            pltpu.VMEM((3, rows, model), jnp.bfloat16),
            dma((ticks, 5, 2, 2)),
            dma((ticks, 5, 2, 2)),
            dma((ticks,)),
            dma((ticks,)),
            dma((8,)),
            dma((8,)),
            dma((11,)),
            dma((11,)),
            dma((PAIRED,)),
            dma((PAIRED,)),
            dma((PAIRED,)),
            dma((PAIRED,)),
            dma,
            dma((3,)),
        ],
        compiler_params=pltpu.CompilerParams(
            collective_id=0, has_side_effects=True, vmem_limit_bytes=50 * 2**20
        ),
        name="gather_and_multiply",
    )(inputs, saved_pre, grad_hidden, weight_in)


def solution(mesh):
    return jax.shard_map(
        local,
        mesh=mesh,
        in_specs=(
            P("col", ("row", "depth")),
            P(("row", "depth"), "col"),
            P(("row", "depth"), "col"),
            P(("row", "depth"), "col"),
        ),
        out_specs=(P("col", ("row", "depth")), P(("row", "depth"), "col")),
        check_vma=False,
    )
```
